32 devices in a mesh: copy: 4 (over y, x), row: 8 (over z, core).
Axes of the slice: x: 2, y: 2, z: 4, core: 2. Of those that a mesh axis runs over, the one named last changes fastest.
Arguments:
- left_proj: bfloat16 [128, 40, 1536], P(None, 'row', 'copy'), may hold values from -6 to 6
- left_gate: bfloat16 [128, 40, 1536], P(None, 'row', 'copy'), may hold values from -8 to 8
- right_factor: bfloat16 [128, 384, 1536], P(None, 'row', 'copy'), may hold values from -6 to 6
- cotangent: bfloat16 [128, 40, 1536], P(None, 'row', 'copy'), may hold values from -0.15625 to 0.15625
- residue_mask: int32 [384], replicated, may hold values 0 or 1
Outputs:
- grad_proj: bfloat16 [128, 40, 1536], P(None, 'row', 'copy')
- grad_gate: bfloat16 [128, 40, 1536], P(None, 'row', 'copy')
- grad_right: bfloat16 [128, 384, 1536], P(None, 'row', 'copy')
The draws below stay inside these ranges and needn't reach their ends.
Inputs may be any that keep to these rules, and one draw needn't show every extreme that they name: `residue_mask`: 1 marks a present residue, 0 a missing one.
All inputs are finite; a program needn't handle non-finite values.
Results may differ from the reference program's by a relative error of at most 0.0049.
Values may be sent and summed in bfloat16 or wider, within the bound.
A program may use at most 64 MiB of HBM per device.

```python
import jax
import jax.numpy as jnp

C = 128
L = 384
ROWS = 40
SYM = 4
N_COPY = 4


def place_ends(array, rng, low, largest):
    index_at = [jax.random.randint(jax.random.fold_in(rng, axis), (), 0, length) for axis, length in enumerate(array.shape)]
    main_axis = array.shape.index(max(array.shape))
    beside = index_at[:main_axis] + [(index_at[main_axis] + 1) % array.shape[main_axis]] + index_at[main_axis + 1:]
    return array.at[tuple(index_at)].set(low).at[tuple(beside)].set(largest)


def steps_of(own_key, shape, cuts, smallest, largest):
    gain, own = 1.0, jax.random.fold_in(own_key, 6)
    for dim, parts in cuts:
        draws = jnp.exp(jax.random.uniform(jax.random.fold_in(own, dim), (parts,), jnp.float32, smallest / len(cuts), largest / len(cuts)))
        gain = gain * jnp.repeat(draws, shape[dim] // parts).reshape([-1 if axis == dim else 1 for axis in range(len(shape))])
    return gain


def gaussian(key, shape, width, limit, cuts=(), dtype=jnp.bfloat16):
    factor_of = steps_of(key, shape, cuts, -0.22, 0.18) if cuts else 1.0
    array = jax.random.normal(key, shape, jnp.float32) * width * factor_of
    return jnp.minimum(jnp.maximum(array, -limit), limit).astype(dtype)


def setup_inputs(seed: int = 0) -> dict:
    key_list = jax.random.split(jax.random.key(seed), 6)
    left_proj = gaussian(key_list[0], (C, ROWS, SYM * L), 1.0, 6.0, ((1, 8), (2, 4)))
    left_gate = gaussian(key_list[1], (C, ROWS, SYM * L), 2.0, 8.0, ((1, 8), (2, 4)))
    right_factor = gaussian(key_list[2], (C, L, SYM * L), 1.0, 6.0, ((1, 8), (2, 4)))
    cotangent = gaussian(key_list[3], (C, ROWS, SYM * L), (L * N_COPY) ** -0.5, 0.15625, ((1, 8), (2, 4)))
    residue_mask = place_ends((jax.random.randint(key_list[4], (L,), 0, 8) < 7).astype(jnp.int32), jax.random.fold_in(key_list[4], 1), 0, 1)
    return {"left_proj": left_proj, "left_gate": left_gate, "right_factor": right_factor, "cotangent": cotangent, "residue_mask": residue_mask}


def reference(left_proj, left_gate, right_factor, cotangent, residue_mask):
    copies = N_COPY
    keep_rows = residue_mask[:ROWS].astype(jnp.float32)
    keep_cols = jnp.tile(residue_mask.astype(jnp.float32), copies)
    keep_both = keep_rows[None, :, None] * keep_cols[None, None, :]
    opened = jax.nn.sigmoid(left_gate.astype(jnp.float32))
    left_factor = (keep_both * opened * left_proj.astype(jnp.float32)).astype(jnp.bfloat16)
    cot_blocks = cotangent.astype(jnp.float32).reshape(C, ROWS, copies, L)
    right_blocks = right_factor.astype(jnp.float32).reshape(C, L, copies, L)
    left_blocks = left_factor.astype(jnp.float32).reshape(C, ROWS, copies, L)
    grad_left = jnp.zeros((C, ROWS, copies, L), jnp.float32)
    grad_right = jnp.zeros((C, L, copies, L), jnp.float32)
    for offset in range(copies):
        shifted_right = jnp.roll(right_blocks, offset, axis=2)
        grad_left = grad_left + jnp.einsum("cij,cjhk->cihk", cot_blocks[:, :, offset], shifted_right)
        shifted_left = jnp.roll(left_blocks, -offset, axis=2)
        grad_right = grad_right + jnp.einsum("cij,cihk->cjhk", cot_blocks[:, :, offset], shifted_left)
    grad_left = grad_left.reshape(C, ROWS, copies * L).astype(jnp.bfloat16).astype(jnp.float32)
    grad_proj = (grad_left * keep_both * opened).astype(jnp.bfloat16)
    grad_gate = (grad_left * keep_both * left_proj.astype(jnp.float32) * opened * (1.0 - opened)).astype(jnp.bfloat16)
    return grad_proj, grad_gate, grad_right.reshape(C, L, copies * L).astype(jnp.bfloat16)
```

```python
import jax
import jax.numpy as jnp
from jax import lax
from jax.experimental import pallas as pl
from jax.experimental.pallas import tpu as pltpu
from jax.sharding import PartitionSpec as P

MESH = pl.DeviceIdType.MESH
ANY = pl.BlockSpec(memory_space=pl.ANY)


def place(copies, rows):
    g, r = lax.axis_index("copy"), lax.axis_index("row")
    core = lax.rem(r, 2)
    return g, r, core, r + 1 - 2 * core


def greet(g, r, others):
    barrier = pltpu.get_barrier_semaphore()
    for device in others:
        pl.semaphore_signal(barrier, inc=1, device_id=device, device_id_type=MESH)
    pl.semaphore_wait(barrier, len(others))


def remote(src, dst, send, recv, device):
    return pltpu.make_async_remote_copy(
        src_ref=src, dst_ref=dst, send_sem=send, recv_sem=recv, device_id=device, device_id_type=MESH
    )


def spread(
    copies, rows, share,
    right, left, cot, right_all, left_all, cot_all,
    left_mid, cot_mid, own, mid_sems, cot_sems, right_sems, row_sems, pair_sems, cot_row_sems,
):
    g, r, core, sibling = place(copies, rows)
    chips = rows // 2
    greet(
        g, r,
        [(lax.rem(g + k, copies), r) for k in range(1, copies)]
        + [(g, lax.rem(r + k, rows)) for k in range(1, rows)],
    )
    local = [
        pltpu.make_async_copy(left.at[:, g], left_mid.at[g], own.at[0]),
        pltpu.make_async_copy(cot.at[g], cot_mid.at[g], own.at[1]),
        pltpu.make_async_copy(right.at[pl.ds(g * share, share)], right_all.at[:, g], own.at[2]),
    ]
    for copy in local:
        copy.start()
    mids, cots, rights = [], [], []
    for k in range(1, copies):
        q = lax.rem(g + k, copies)
        mids.append(remote(left.at[:, q], left_mid.at[g], mid_sems.at[0, k], mid_sems.at[1, k], (q, r)))
        cots.append(remote(cot.at[q], cot_mid.at[g], cot_sems.at[0, k], cot_sems.at[1, k], (q, r)))
        rights.append(
            remote(
                right.at[pl.ds(q * share, share)], right_all.at[:, g],
                right_sems.at[0, k], right_sems.at[1, k], (q, r),
            )
        )
    for copy in mids + cots + rights:
        copy.start()
    local[0].wait()
    for copy in mids:
        copy.wait_recv()
    along = []
    for k in range(1, chips):
        peer = lax.rem(r + 2 * k, rows)
        along.append(remote(left_mid, left_all.at[r], row_sems.at[0, k], row_sems.at[1, k], (g, peer)))
    pairs = [remote(left_mid, left_all.at[r], pair_sems.at[0, 0], pair_sems.at[1, 0], (g, sibling))]
    keep = pltpu.make_async_copy(left_mid, left_all.at[r], own.at[3])
    for copy in along + pairs + [keep]:
        copy.start()
    local[1].wait()
    for copy in cots:
        copy.wait_recv()
    cot_rows = []
    for k in range(1, rows):
        peer = lax.rem(r + k, rows)
        cot_rows.append(
            remote(cot_mid.at[:, peer], cot_all.at[r], cot_row_sems.at[0, k], cot_row_sems.at[1, k], (g, peer))
        )
    keep_cot = pltpu.make_async_copy(cot_mid.at[:, r], cot_all.at[r], own.at[4])
    for copy in cot_rows + [keep_cot]:
        copy.start()
    for k in range(1, chips):
        along[k - 1].wait_recv()
        source = lax.rem(r + rows - 2 * k, rows)
        pairs.append(
            remote(
                left_all.at[source], left_all.at[source],
                pair_sems.at[0, k], pair_sems.at[1, k], (g, sibling),
            )
        )
        pairs[-1].start()
    for copy in pairs + cot_rows + rights:
        copy.wait_recv()
    for copy in mids + cots + rights + along + pairs + cot_rows:
        copy.wait_send()
    local[2].wait()
    keep.wait()
    keep_cot.wait()


def collect(
    copies, rows, share,
    back, part, right_out, left_out,
    mine, pair_in, total, chip_in, done, own, back_sems, pair_sems, row_sems, out_sems,
):
    g, r, core, sibling = place(copies, rows)
    chips = rows // 2
    chip = r // 2
    greet(
        g, r,
        [(lax.rem(g + k, copies), r) for k in range(1, copies)]
        + [(g, lax.rem(r + 2 * k, rows)) for k in range(1, chips)]
        + [(g, sibling)],
    )
    pairs, loads = [], []
    for z in range(chips):
        pairs.append(
            remote(part.at[2 * z + 1 - core], pair_in.at[z], pair_sems.at[0, z], pair_sems.at[1, z], (g, sibling))
        )
        loads.append(pltpu.make_async_copy(part.at[2 * z + core], mine.at[z], own.at[z]))
    backs = []
    for k in range(1, copies):
        q = lax.rem(g + k, copies)
        backs.append(
            remote(
                back.at[:, q], right_out.at[pl.ds(g * share, share)],
                back_sems.at[0, k], back_sems.at[1, k], (q, r),
            )
        )
    keep = pltpu.make_async_copy(back.at[:, g], right_out.at[pl.ds(g * share, share)], own.at[chips])
    for copy in pairs + loads + backs + [keep]:
        copy.start()
    for z in range(chips):
        pairs[z].wait_recv()
        loads[z].wait()
    rights = []
    for k in range(1, chips):
        z = lax.rem(chip + k, chips)
        total[z] = (mine[z].astype(jnp.float32) + pair_in[z].astype(jnp.float32)).astype(total.dtype)
        rights.append(
            remote(total.at[z], chip_in.at[k], row_sems.at[0, k], row_sems.at[1, k], (g, 2 * z + core))
        )
        rights[-1].start()
    for copy in rights:
        copy.wait_recv()
    rest = mine[chip].astype(jnp.float32) + pair_in[chip].astype(jnp.float32)
    for k in range(1, chips):
        rest = rest + chip_in[k].astype(jnp.float32)
    done[...] = rest.astype(done.dtype).reshape(done.shape)
    lefts = []
    for k in range(1, copies):
        q = lax.rem(g + k, copies)
        lefts.append(remote(done.at[q], left_out.at[:, g], out_sems.at[0, k], out_sems.at[1, k], (q, r)))
    keep_left = pltpu.make_async_copy(done.at[g], left_out.at[:, g], own.at[chips + 1])
    for copy in lefts + [keep_left]:
        copy.start()
    for copy in backs + lefts:
        copy.wait_recv()
    for copy in pairs + backs + rights + lefts:
        copy.wait_send()
    keep.wait()
    keep_left.wait()


def sems(*shape):
    return pltpu.SemaphoreType.DMA(shape)


def on_device(left_proj, left_gate, right_factor, cotangent, residue_mask):
    copies = lax.axis_size("copy")
    rows = lax.axis_size("row")
    row_here = lax.axis_index("row")
    channels, held, length = left_proj.shape
    share = channels // copies
    block = right_factor.shape[1]
    bf16 = jnp.bfloat16
    keep_rows = lax.dynamic_slice_in_dim(residue_mask, row_here * held, held).astype(jnp.float32)
    keep_cols = residue_mask.astype(jnp.float32)
    keep_both = keep_rows[None, :, None] * keep_cols[None, None, :]
    opened = jax.nn.sigmoid(left_gate.astype(jnp.float32))
    left_factor = (keep_both * opened * left_proj.astype(jnp.float32)).astype(bf16)
    left_in = left_factor.transpose(1, 0, 2).reshape(held, copies, share, length)

    size = held * share * block
    tall = -(-size // 2048) * 16
    cot = cotangent.reshape(copies, share, held, rows, block).transpose(0, 3, 2, 1, 4)
    cot = jnp.pad(cot.reshape(copies, rows, size), ((0, 0), (0, 0), (0, tall * 128 - size)))
    cot = cot.reshape(copies, rows, tall, 128)

    def kernel(body):
        return lambda *refs: body(copies, rows, share, *refs)

    chips = rows // 2
    right, left, cot = pl.pallas_call(
        kernel(spread),
        out_shape=(
            jax.ShapeDtypeStruct((share, copies, block, length), bf16),
            jax.ShapeDtypeStruct((rows, copies, held, share, length), bf16),
            jax.ShapeDtypeStruct((rows, copies, tall, 128), bf16),
        ),
        in_specs=[ANY] * 3,
        out_specs=(ANY,) * 3,
        scratch_shapes=[
            pltpu.VMEM((copies, held, share, length), bf16),
            pltpu.VMEM((copies, rows, tall, 128), bf16),
            sems(5),
            sems(2, copies),
            sems(2, copies),
            sems(2, copies),
            sems(2, chips),
            sems(2, chips),
            sems(2, rows),
        ],
        compiler_params=pltpu.CompilerParams(
            collective_id=0, has_side_effects=True, vmem_limit_bytes=48 << 20
        ),
    )(right_factor, left_in, cot)

    cot = cot.reshape(rows, copies, tall * 128)[:, :, :size].reshape(rows, copies, held, share, block)
    cot = cot.transpose(3, 0, 1, 2, 4)
    matrix = jnp.concatenate(
        [
            jnp.roll(cot, source, axis=2).reshape(share, rows * copies * held, block)
            for source in range(copies)
        ],
        axis=2,
    )
    left = left.reshape(rows * copies * held, share, length).transpose(1, 0, 2)
    back = jnp.einsum("cij,cik->cjk", matrix, left, preferred_element_type=jnp.float32).astype(bf16)
    back = back.reshape(share, copies, block, length)
    right = right.reshape(share, copies * block, length)
    part = jnp.einsum("cij,cjk->cik", matrix, right, preferred_element_type=jnp.float32).astype(bf16)
    part = part.transpose(1, 0, 2).reshape(rows, copies * held, share, length)

    slab = (copies * held, share, length)
    grad_right, left_sum = pl.pallas_call(
        kernel(collect),
        out_shape=(
            jax.ShapeDtypeStruct(right_factor.shape, bf16),
            jax.ShapeDtypeStruct((held, copies, share, length), bf16),
        ),
        in_specs=[ANY] * 2,
        out_specs=(ANY,) * 2,
        scratch_shapes=[
            pltpu.VMEM((chips,) + slab, bf16),
            pltpu.VMEM((chips,) + slab, bf16),
            pltpu.VMEM((chips,) + slab, bf16),
            pltpu.VMEM((chips,) + slab, bf16),
            pltpu.VMEM((copies, held, share, length), bf16),
            sems(chips + 2),
            sems(2, copies),
            sems(2, chips),
            sems(2, chips),
            sems(2, copies),
        ],
        compiler_params=pltpu.CompilerParams(
            collective_id=1, has_side_effects=True, vmem_limit_bytes=48 << 20
        ),
    )(back, part)

    left_wide = left_sum.reshape(held, channels, length).transpose(1, 0, 2).astype(jnp.float32)
    grad_proj = (left_wide * keep_both * opened).astype(bf16)
    grad_gate = (
        left_wide * keep_both * left_proj.astype(jnp.float32) * opened * (1.0 - opened)
    ).astype(bf16)
    return (grad_proj, grad_gate, grad_right)


def solution(mesh):
    spec = P(None, "row", "copy")
    return jax.shard_map(
        on_device,
        mesh=mesh,
        in_specs=(spec, spec, spec, spec, P()),
        out_specs=(spec, spec, spec),
        check_vma=False,
    )
```

```python
import jax
import jax.numpy as jnp
from jax import lax
from jax.experimental import pallas as pl
from jax.experimental.pallas import tpu as pltpu
from jax.sharding import PartitionSpec as P

MESH = pl.DeviceIdType.MESH
ANY = pl.BlockSpec(memory_space=pl.ANY)


def place(copies, rows):
    g, r = lax.axis_index("copy"), lax.axis_index("row")
    core = lax.rem(r, 2)
    return g, r, core, r + 1 - 2 * core


def greet(g, r, others):
    barrier = pltpu.get_barrier_semaphore()
    for device in others:
        pl.semaphore_signal(barrier, inc=1, device_id=device, device_id_type=MESH)
    pl.semaphore_wait(barrier, len(others))


def remote(src, dst, send, recv, device):
    return pltpu.make_async_remote_copy(
        src_ref=src, dst_ref=dst, send_sem=send, recv_sem=recv, device_id=device, device_id_type=MESH
    )


def spread(
    copies, rows, share,
    right, left, cot, right_all, left_all, cot_all,
    left_mid, cot_mid, own, mid_sems, cot_sems, right_sems, row_sems, pair_sems, cot_row_sems,
):
    g, r, core, sibling = place(copies, rows)
    chips = rows // 2
    greet(
        g, r,
        [(lax.rem(g + k, copies), r) for k in range(1, copies)]
        + [(g, lax.rem(r + k, rows)) for k in range(1, rows)],
    )
    local = [
        pltpu.make_async_copy(left.at[:, g], left_mid.at[g], own.at[0]),
        pltpu.make_async_copy(cot.at[g], cot_mid.at[g], own.at[1]),
        pltpu.make_async_copy(right.at[pl.ds(g * share, share)], right_all.at[:, g], own.at[2]),
    ]
    for copy in local:
        copy.start()
    mids, cots, rights = [], [], []
    for k in range(1, copies):
        q = lax.rem(g + k, copies)
        mids.append(remote(left.at[:, q], left_mid.at[g], mid_sems.at[0, k], mid_sems.at[1, k], (q, r)))
        cots.append(remote(cot.at[q], cot_mid.at[g], cot_sems.at[0, k], cot_sems.at[1, k], (q, r)))
        rights.append(
            remote(
                right.at[pl.ds(q * share, share)], right_all.at[:, g],
                right_sems.at[0, k], right_sems.at[1, k], (q, r),
            )
        )
    for copy in mids + cots + rights:
        copy.start()
    local[0].wait()
    for copy in mids:
        copy.wait_recv()
    along = []
    for k in range(1, chips):
        peer = lax.rem(r + 2 * k, rows)
        along.append(remote(left_mid, left_all.at[r], row_sems.at[0, k], row_sems.at[1, k], (g, peer)))
    pairs = [remote(left_mid, left_all.at[r], pair_sems.at[0, 0], pair_sems.at[1, 0], (g, sibling))]
    keep = pltpu.make_async_copy(left_mid, left_all.at[r], own.at[3])
    for copy in along + pairs + [keep]:
        copy.start()
    local[1].wait()
    for copy in cots:
        copy.wait_recv()
    cot_rows = []
    for k in range(1, rows):
        peer = lax.rem(r + k, rows)
        cot_rows.append(
            remote(cot_mid.at[:, peer], cot_all.at[r], cot_row_sems.at[0, k], cot_row_sems.at[1, k], (g, peer))
        )
    keep_cot = pltpu.make_async_copy(cot_mid.at[:, r], cot_all.at[r], own.at[4])
    for copy in cot_rows + [keep_cot]:
        copy.start()
    for k in range(1, chips):
        along[k - 1].wait_recv()
        source = lax.rem(r + rows - 2 * k, rows)
        pairs.append(
            remote(
                left_all.at[source], left_all.at[source],
                pair_sems.at[0, k], pair_sems.at[1, k], (g, sibling),
            )
        )
        pairs[-1].start()
    for copy in pairs + cot_rows + rights:
        copy.wait_recv()
    for copy in mids + cots + rights + along + pairs + cot_rows:
        copy.wait_send()
    local[2].wait()
    keep.wait()
    keep_cot.wait()


def collect(
    copies, rows, share,
    back, matrix, right, right_out, left_out,
    factor, held_matrix, part, pair_in, chip_in, done,
    own, back_sems, pair_sems, row_sems, out_sems,
):
    g, r, core, sibling = place(copies, rows)
    chips = rows // 2
    chip = r // 2
    loads = [
        pltpu.make_async_copy(matrix, held_matrix, own.at[0]),
        pltpu.make_async_copy(right, factor, own.at[1]),
    ]
    for copy in loads:
        copy.start()
    greet(
        g, r,
        [(lax.rem(g + k, copies), r) for k in range(1, copies)]
        + [(g, lax.rem(r + 2 * k, rows)) for k in range(1, chips)]
        + [(g, sibling)],
    )
    backs = []
    for k in range(1, copies):
        q = lax.rem(g + k, copies)
        backs.append(
            remote(
                back.at[:, q], right_out.at[pl.ds(g * share, share)],
                back_sems.at[0, k], back_sems.at[1, k], (q, r),
            )
        )
    keep = pltpu.make_async_copy(back.at[:, g], right_out.at[pl.ds(g * share, share)], own.at[2])
    for copy in backs + [keep]:
        copy.start()
    for copy in loads:
        copy.wait()
    step = 16 if share % 16 == 0 else share
    groups, tall = held_matrix.shape[1], held_matrix.shape[2]
    slab = part.shape[1:]

    def multiply(group, carry):
        for first in range(0, share, step):
            product = lax.dot_general(
                held_matrix[first : first + step, group],
                factor[first : first + step],
                (((2,), (1,)), ((0,), (0,))),
                preferred_element_type=jnp.float32,
            )
            turned = jnp.swapaxes(product.astype(part.dtype), 0, 1)
            part[pl.ds(group * (rows // groups), rows // groups), :, first : first + step, :] = (
                turned.reshape(rows // groups, slab[0], step, slab[2])
            )
        return carry

    lax.fori_loop(0, groups, multiply, 0)
    pairs = []
    for k in range(chips):
        z = lax.rem(chip + 1 + k, chips)
        pairs.append(
            remote(part.at[2 * z + 1 - core], pair_in.at[k], pair_sems.at[0, k], pair_sems.at[1, k], (g, sibling))
        )
        pairs[-1].start()
    rights = []
    for k in range(1, chips):
        z = lax.rem(chip + k, chips)
        pairs[k - 1].wait_recv()
        mine = part[2 * z + core].astype(jnp.float32) + pair_in[k - 1].astype(jnp.float32)
        part[2 * z + core] = mine.astype(part.dtype)
        rights.append(
            remote(part.at[2 * z + core], chip_in.at[k], row_sems.at[0, k], row_sems.at[1, k], (g, 2 * z + core))
        )
        rights[-1].start()
    pairs[chips - 1].wait_recv()
    for copy in rights:
        copy.wait_recv()
    rest = part[r].astype(jnp.float32) + pair_in[chips - 1].astype(jnp.float32)
    for k in range(1, chips):
        rest = rest + chip_in[k].astype(jnp.float32)
    done[...] = rest.astype(done.dtype).reshape(done.shape)
    lefts = []
    for k in range(1, copies):
        q = lax.rem(g + k, copies)
        lefts.append(remote(done.at[q], left_out.at[:, g], out_sems.at[0, k], out_sems.at[1, k], (q, r)))
    keep_left = pltpu.make_async_copy(done.at[g], left_out.at[:, g], own.at[3])
    for copy in lefts + [keep_left]:
        copy.start()
    for copy in backs + lefts:
        copy.wait_recv()
    for copy in pairs + backs + rights + lefts:
        copy.wait_send()
    keep.wait()
    keep_left.wait()


def sems(*shape):
    return pltpu.SemaphoreType.DMA(shape)


def on_device(left_proj, left_gate, right_factor, cotangent, residue_mask):
    copies = lax.axis_size("copy")
    rows = lax.axis_size("row")
    row_here = lax.axis_index("row")
    channels, held, length = left_proj.shape
    share = channels // copies
    block = right_factor.shape[1]
    bf16 = jnp.bfloat16
    keep_rows = lax.dynamic_slice_in_dim(residue_mask, row_here * held, held).astype(jnp.float32)
    keep_cols = residue_mask.astype(jnp.float32)
    keep_both = keep_rows[None, :, None] * keep_cols[None, None, :]
    opened = jax.nn.sigmoid(left_gate.astype(jnp.float32))
    left_factor = (keep_both * opened * left_proj.astype(jnp.float32)).astype(bf16)
    left_in = left_factor.transpose(1, 0, 2).reshape(held, copies, share, length)

    size = held * share * block
    tall = -(-size // 2048) * 16
    cot = cotangent.reshape(copies, share, held, rows, block).transpose(0, 3, 2, 1, 4)
    cot = jnp.pad(cot.reshape(copies, rows, size), ((0, 0), (0, 0), (0, tall * 128 - size)))
    cot = cot.reshape(copies, rows, tall, 128)

    def kernel(body):
        return lambda *refs: body(copies, rows, share, *refs)

    chips = rows // 2
    right, left, cot = pl.pallas_call(
        kernel(spread),
        out_shape=(
            jax.ShapeDtypeStruct((share, copies, block, length), bf16),
            jax.ShapeDtypeStruct((rows, copies, held, share, length), bf16),
            jax.ShapeDtypeStruct((rows, copies, tall, 128), bf16),
        ),
        in_specs=[ANY] * 3,
        out_specs=(ANY,) * 3,
        scratch_shapes=[
            pltpu.VMEM((copies, held, share, length), bf16),
            pltpu.VMEM((copies, rows, tall, 128), bf16),
            sems(5),
            sems(2, copies),
            sems(2, copies),
            sems(2, copies),
            sems(2, chips),
            sems(2, chips),
            sems(2, rows),
        ],
        compiler_params=pltpu.CompilerParams(
            collective_id=0, has_side_effects=True, vmem_limit_bytes=8 << 20
        ),
    )(right_factor, left_in, cot)

    cot = cot.reshape(rows, copies, tall * 128)[:, :, :size].reshape(rows, copies, held, share, block)
    cot = cot.transpose(3, 0, 1, 2, 4)
    matrix = jnp.concatenate(
        [
            jnp.roll(cot, source, axis=2).reshape(share, rows * copies * held, block)
            for source in range(copies)
        ],
        axis=2,
    )
    left = left.reshape(rows * copies * held, share, length).transpose(1, 0, 2)
    back = jnp.einsum("cij,cik->cjk", matrix, left, preferred_element_type=jnp.float32).astype(bf16)
    back = back.reshape(share, copies, block, length)
    right = right.reshape(share, copies * block, length)
    groups = rows // 8 if rows % 8 == 0 else 1
    grouped = matrix.reshape(share, groups, matrix.shape[1] // groups, copies * block)

    slab = (copies * held, share, length)
    slab_bytes = 2 * copies * held * share * length
    grad_right, left_sum = pl.pallas_call(
        kernel(collect),
        out_shape=(
            jax.ShapeDtypeStruct(right_factor.shape, bf16),
            jax.ShapeDtypeStruct((held, copies, share, length), bf16),
        ),
        in_specs=[ANY] * 3,
        out_specs=(ANY,) * 2,
        scratch_shapes=[
            pltpu.VMEM(right.shape, bf16),
            pltpu.VMEM(grouped.shape, bf16),
            pltpu.VMEM((rows,) + slab, bf16),
            pltpu.VMEM((chips,) + slab, bf16),
            pltpu.VMEM((chips,) + slab, bf16),
            pltpu.VMEM((copies, held, share, length), bf16),
            sems(4),
            sems(2, copies),
            sems(2, chips),
            sems(2, chips),
            sems(2, copies),
        ],
        compiler_params=pltpu.CompilerParams(
            collective_id=1, has_side_effects=True,
            vmem_limit_bytes=(24 << 20) + 2 * rows * slab_bytes,
        ),
    )(back, grouped, right)

    left_wide = left_sum.reshape(held, channels, length).transpose(1, 0, 2).astype(jnp.float32)
    grad_proj = (left_wide * keep_both * opened).astype(bf16)
    grad_gate = (
        left_wide * keep_both * left_proj.astype(jnp.float32) * opened * (1.0 - opened)
    ).astype(bf16)
    return (grad_proj, grad_gate, grad_right)


def solution(mesh):
    spec = P(None, "row", "copy")
    return jax.shard_map(
        on_device,
        mesh=mesh,
        in_specs=(spec, spec, spec, spec, P()),
        out_specs=(spec, spec, spec),
        check_vma=False,
    )
```

```python
import jax
import jax.numpy as jnp
from jax import lax
from jax.experimental import pallas as pl
from jax.experimental.pallas import tpu as pltpu
from jax.sharding import PartitionSpec as P

MESH = pl.DeviceIdType.MESH
ANY = pl.BlockSpec(memory_space=pl.ANY)


def place(copies, rows):
    g, r = lax.axis_index("copy"), lax.axis_index("row")
    core = lax.rem(r, 2)
    return g, r, core, r + 1 - 2 * core


def greet(g, r, others):
    barrier = pltpu.get_barrier_semaphore()
    for device in others:
        pl.semaphore_signal(barrier, inc=1, device_id=device, device_id_type=MESH)
    pl.semaphore_wait(barrier, len(others))


def remote(src, dst, send, recv, device):
    return pltpu.make_async_remote_copy(
        src_ref=src, dst_ref=dst, send_sem=send, recv_sem=recv, device_id=device, device_id_type=MESH
    )


def spread(
    copies, rows, share,
    left, cot, left_all, cot_all,
    left_mid, cot_mid, own, mid_sems, cot_sems, row_sems, pair_sems, cot_row_sems,
):
    g, r, core, sibling = place(copies, rows)
    chips = rows // 2
    greet(
        g, r,
        [(lax.rem(g + k, copies), r) for k in range(1, copies)]
        + [(g, lax.rem(r + k, rows)) for k in range(1, rows)],
    )
    local = [
        pltpu.make_async_copy(left.at[:, g], left_mid.at[g], own.at[0]),
        pltpu.make_async_copy(cot.at[g], cot_mid.at[g], own.at[1]),
    ]
    for copy in local:
        copy.start()
    mids, cots = [], []
    for k in range(1, copies):
        q = lax.rem(g + k, copies)
        mids.append(remote(left.at[:, q], left_mid.at[g], mid_sems.at[0, k], mid_sems.at[1, k], (q, r)))
        cots.append(remote(cot.at[q], cot_mid.at[g], cot_sems.at[0, k], cot_sems.at[1, k], (q, r)))
    for copy in mids + cots:
        copy.start()
    local[0].wait()
    for copy in mids:
        copy.wait_recv()
    along = []
    for k in range(1, chips):
        peer = lax.rem(r + 2 * k, rows)
        along.append(remote(left_mid, left_all.at[r], row_sems.at[0, k], row_sems.at[1, k], (g, peer)))
    pairs = [remote(left_mid, left_all.at[r], pair_sems.at[0, 0], pair_sems.at[1, 0], (g, sibling))]
    keep = pltpu.make_async_copy(left_mid, left_all.at[r], own.at[3])
    for copy in along + pairs + [keep]:
        copy.start()
    local[1].wait()
    for copy in cots:
        copy.wait_recv()
    cot_rows = []
    for k in range(1, rows):
        peer = lax.rem(r + k, rows)
        cot_rows.append(
            remote(cot_mid.at[:, peer], cot_all.at[r], cot_row_sems.at[0, k], cot_row_sems.at[1, k], (g, peer))
        )
    keep_cot = pltpu.make_async_copy(cot_mid.at[:, r], cot_all.at[r], own.at[4])
    for copy in cot_rows + [keep_cot]:
        copy.start()
    for k in range(1, chips):
        along[k - 1].wait_recv()
        source = lax.rem(r + rows - 2 * k, rows)
        pairs.append(
            remote(
                left_all.at[source], left_all.at[source],
                pair_sems.at[0, k], pair_sems.at[1, k], (g, sibling),
            )
        )
        pairs[-1].start()
    for copy in pairs + cot_rows:
        copy.wait_recv()
    for copy in mids + cots + along + pairs + cot_rows:
        copy.wait_send()
    keep.wait()
    keep_cot.wait()


def collect(
    copies, rows, share,
    back, matrix, right, *refs,
):
    arrived, refs = refs[: copies - 1], refs[copies - 1 :]
    (
    right_out, left_out,
    factor, held_matrix, part, pair_in, chip_in, done,
    own, back_sems, pair_sems, row_sems, out_sems,
    ) = refs
    g, r, core, sibling = place(copies, rows)
    chips = rows // 2
    chip = r // 2
    loads = [
        pltpu.make_async_copy(matrix, held_matrix, own.at[0]),
        pltpu.make_async_copy(right.at[pl.ds(g * share, share)], factor.at[0], own.at[1]),
    ] + [
        pltpu.make_async_copy(arrived[k - 1], factor.at[k], own.at[3 + k])
        for k in range(1, copies)
    ]
    for copy in loads:
        copy.start()
    greet(
        g, r,
        [(lax.rem(g + k, copies), r) for k in range(1, copies)]
        + [(g, lax.rem(r + 2 * k, rows)) for k in range(1, chips)]
        + [(g, sibling)],
    )
    backs = []
    for k in range(1, copies):
        q = lax.rem(g + k, copies)
        backs.append(
            remote(
                back.at[:, q], right_out.at[pl.ds(g * share, share)],
                back_sems.at[0, k], back_sems.at[1, k], (q, r),
            )
        )
    keep = pltpu.make_async_copy(back.at[:, g], right_out.at[pl.ds(g * share, share)], own.at[2])
    for copy in backs + [keep]:
        copy.start()
    for copy in loads:
        copy.wait()
    step = 16 if share % 16 == 0 else share
    groups, depth = held_matrix.shape[1], factor.shape[2]
    slab = part.shape[1:]

    def multiply(group, carry):
        for first in range(0, share, step):
            product = 0.0
            for source in range(copies):
                product = product + lax.dot_general(
                    held_matrix[first : first + step, group, :, source * depth : (source + 1) * depth],
                    factor[lax.rem(g + copies - source, copies), first : first + step],
                    (((2,), (1,)), ((0,), (0,))),
                    preferred_element_type=jnp.float32,
                )
            turned = jnp.swapaxes(product.astype(part.dtype), 0, 1)
            part[pl.ds(group * (rows // groups), rows // groups), :, first : first + step, :] = (
                turned.reshape(rows // groups, slab[0], step, slab[2])
            )
        return carry

    lax.fori_loop(0, groups, multiply, 0)
    pairs = []
    for k in range(chips):
        z = lax.rem(chip + 1 + k, chips)
        pairs.append(
            remote(part.at[2 * z + 1 - core], pair_in.at[k], pair_sems.at[0, k], pair_sems.at[1, k], (g, sibling))
        )
        pairs[-1].start()
    rights = []
    for k in range(1, chips):
        z = lax.rem(chip + k, chips)
        pairs[k - 1].wait_recv()
        mine = part[2 * z + core].astype(jnp.float32) + pair_in[k - 1].astype(jnp.float32)
        part[2 * z + core] = mine.astype(part.dtype)
        rights.append(
            remote(part.at[2 * z + core], chip_in.at[k], row_sems.at[0, k], row_sems.at[1, k], (g, 2 * z + core))
        )
        rights[-1].start()
    pairs[chips - 1].wait_recv()
    for copy in rights:
        copy.wait_recv()
    rest = part[r].astype(jnp.float32) + pair_in[chips - 1].astype(jnp.float32)
    for k in range(1, chips):
        rest = rest + chip_in[k].astype(jnp.float32)
    done[...] = rest.astype(done.dtype).reshape(done.shape)
    lefts = []
    for k in range(1, copies):
        q = lax.rem(g + k, copies)
        lefts.append(remote(done.at[q], left_out.at[:, g], out_sems.at[0, k], out_sems.at[1, k], (q, r)))
    keep_left = pltpu.make_async_copy(done.at[g], left_out.at[:, g], own.at[3])
    for copy in lefts + [keep_left]:
        copy.start()
    for copy in backs + lefts:
        copy.wait_recv()
    for copy in pairs + backs + rights + lefts:
        copy.wait_send()
    keep.wait()
    keep_left.wait()


def sems(*shape):
    return pltpu.SemaphoreType.DMA(shape)


def on_device(left_proj, left_gate, right_factor, cotangent, residue_mask):
    copies = lax.axis_size("copy")
    rows = lax.axis_size("row")
    row_here = lax.axis_index("row")
    channels, held, length = left_proj.shape
    share = channels // copies
    block = right_factor.shape[1]
    bf16 = jnp.bfloat16
    keep_rows = lax.dynamic_slice_in_dim(residue_mask, row_here * held, held).astype(jnp.float32)
    keep_cols = residue_mask.astype(jnp.float32)
    keep_both = keep_rows[None, :, None] * keep_cols[None, None, :]
    opened = jax.nn.sigmoid(left_gate.astype(jnp.float32))
    left_factor = (keep_both * opened * left_proj.astype(jnp.float32)).astype(bf16)
    left_in = left_factor.transpose(1, 0, 2).reshape(held, copies, share, length)

    copy_here = lax.axis_index("copy")
    arrived = []
    for k in range(1, copies):
        start = (copy_here + k) % copies * share
        piece = lax.dynamic_slice_in_dim(right_factor, start, share)
        arrived.append(lax.ppermute(piece, "copy", [(d, (d + k) % copies) for d in range(copies)]))

    size = held * share * block
    tall = -(-size // 2048) * 16
    cot = cotangent.reshape(copies, share, held, rows, block).transpose(0, 3, 2, 1, 4)
    cot = jnp.pad(cot.reshape(copies, rows, size), ((0, 0), (0, 0), (0, tall * 128 - size)))
    cot = cot.reshape(copies, rows, tall, 128)

    def kernel(body):
        return lambda *refs: body(copies, rows, share, *refs)

    chips = rows // 2
    left, cot = pl.pallas_call(
        kernel(spread),
        out_shape=(
            jax.ShapeDtypeStruct((rows, copies, held, share, length), bf16),
            jax.ShapeDtypeStruct((rows, copies, tall, 128), bf16),
        ),
        in_specs=[ANY] * 2,
        out_specs=(ANY,) * 2,
        scratch_shapes=[
            pltpu.VMEM((copies, held, share, length), bf16),
            pltpu.VMEM((copies, rows, tall, 128), bf16),
            sems(5),
            sems(2, copies),
            sems(2, copies),
            sems(2, chips),
            sems(2, chips),
            sems(2, rows),
        ],
        cost_estimate=pl.CostEstimate(flops=0, bytes_accessed=180_000_000, transcendentals=0),
        compiler_params=pltpu.CompilerParams(
            collective_id=0, has_side_effects=True, vmem_limit_bytes=8 << 20
        ),
    )(left_in, cot)

    cot = cot.reshape(rows, copies, tall * 128)[:, :, :size].reshape(rows, copies, held, share, block)
    cot = cot.transpose(3, 0, 1, 2, 4)
    blocks = [
        jnp.roll(cot, source, axis=2).reshape(share, rows * copies * held, block)
        for source in range(copies)
    ]
    matrix = jnp.concatenate(blocks, axis=2)
    left = left.reshape(rows * copies * held, share, length).transpose(1, 0, 2)
    back = jnp.einsum("cij,cik->cjk", matrix, left, preferred_element_type=jnp.float32).astype(bf16)
    back = back.reshape(share, copies, block, length)
    groups = rows // 8 if rows % 8 == 0 else 1
    grouped = matrix.reshape(share, groups, -1, copies * block)

    slab = (copies * held, share, length)
    slab_bytes = 2 * copies * held * share * length
    grad_right, left_sum = pl.pallas_call(
        kernel(collect),
        out_shape=(
            jax.ShapeDtypeStruct(right_factor.shape, bf16),
            jax.ShapeDtypeStruct((held, copies, share, length), bf16),
        ),
        in_specs=[ANY] * (copies + 2),
        out_specs=(ANY,) * 2,
        scratch_shapes=[
            pltpu.VMEM((copies, share, block, length), bf16),
            pltpu.VMEM(grouped.shape, bf16),
            pltpu.VMEM((rows,) + slab, bf16),
            pltpu.VMEM((chips,) + slab, bf16),
            pltpu.VMEM((chips,) + slab, bf16),
            pltpu.VMEM((copies, held, share, length), bf16),
            sems(3 + copies),
            sems(2, copies),
            sems(2, chips),
            sems(2, chips),
            sems(2, copies),
        ],
        compiler_params=pltpu.CompilerParams(
            collective_id=1, has_side_effects=True,
            vmem_limit_bytes=(24 << 20) + 2 * rows * slab_bytes,
        ),
    )(back, grouped, right_factor, *arrived)

    left_wide = left_sum.reshape(held, channels, length).transpose(1, 0, 2).astype(jnp.float32)
    grad_proj = (left_wide * keep_both * opened).astype(bf16)
    grad_gate = (
        left_wide * keep_both * left_proj.astype(jnp.float32) * opened * (1.0 - opened)
    ).astype(bf16)
    return (grad_proj, grad_gate, grad_right)


def solution(mesh):
    spec = P(None, "row", "copy")
    return jax.shard_map(
        on_device,
        mesh=mesh,
        in_specs=(spec, spec, spec, spec, P()),
        out_specs=(spec, spec, spec),
        check_vma=False,
    )
```
